256 devices in a mesh: dp: 16 (over z_hi, y, core), space: 16 (over x, z_lo).
Axes of the slice: x: 4, y: 4, z: 8 (z_hi: 2, z_lo: 4; z = z_hi * 4 + z_lo), core: 2. Of those that a mesh axis runs over, the one named last changes fastest.
Arguments:
- state: bfloat16 [16, 5, 256, 96, 192], P('dp', None, 'space'), may hold values from -6 to 6
- cotangent: bfloat16 [16, 5, 256, 96, 192], P('dp', None, 'space'), may hold values from -24 to 24
- x_operator: bfloat16 [256, 256], replicated, may hold values from -0.375 to 0.375
- y_operator: bfloat16 [96, 96], replicated, may hold values from -0.625 to 0.625
- z_operator: bfloat16 [192, 192], replicated, may hold values from -0.4375 to 0.4375
- w_in: bfloat16 [64, 20], replicated, may hold values from -1.25 to 1.25
- b_in: float32 [64], replicated, may hold values from -3 to 3
- w_out: bfloat16 [5, 64], replicated, may hold values from -0.75 to 0.75
- b_out: float32 [5], replicated, may hold values from -3 to 3
Outputs:
- new_state: bfloat16 [16, 5, 256, 96, 192], P('dp', None, 'space')
- state_grad: bfloat16 [16, 5, 256, 96, 192], P('dp', None, 'space')
- w_in_grad: float32 [64, 20], replicated
- b_in_grad: float32 [64], replicated
- w_out_grad: float32 [5, 64], replicated
- b_out_grad: float32 [5], replicated
The draws below stay inside these ranges and needn't reach their ends.
All inputs are finite; a program needn't handle non-finite values.
Results may differ from the reference program's by a relative error of at most 0.012.
Values may be sent and summed in bfloat16 or wider, within the bound.
A program may use at most 128 MiB of HBM per device.

```python
import math
import jax
import jax.numpy as jnp
from jax import lax

FIELDS = 5
NX = 256
NY = 96
NZ = 192
HIDDEN_SIZE = 64
FEATURES = 20
TRAJ = 16


def block_levels(key, dims, pieces, smallest, top_value):
    factor_of = 1.0
    for position, parts in pieces:
        heights = jax.random.uniform(jax.random.fold_in(jax.random.fold_in(key, 6), position), (parts,), jnp.float32, smallest / len(pieces), top_value / len(pieces))
        factor_of = factor_of * jnp.repeat(jnp.exp(heights), dims[position] // parts).reshape((-1,) + (1,) * (len(dims) - 1 - position))
    return factor_of


def bell_draw(own_key, dims, deviation, limit, split=(), held_as=jnp.bfloat16):
    result = jax.random.normal(own_key, dims, jnp.float32) * deviation
    if len(split) > 0:
        result = block_levels(own_key, dims, split, -0.22, 0.18) * result
    return jnp.clip(result, min=-limit, max=limit).astype(held_as)


def setup_inputs(seed: int = 0) -> dict:
    key_of = jax.random.split(jax.random.key(seed), 10)
    state = bell_draw(key_of[0], (TRAJ, FIELDS, NX, NY, NZ), 1.0, 6.0, ((0, 16), (2, 16)))
    cotangent = bell_draw(key_of[1], (TRAJ, FIELDS, NX, NY, NZ), 4.0, 24.0, ((0, 16), (2, 16)))
    x_operator = bell_draw(key_of[2], (NX, NX), NX ** -0.5, 0.375)
    y_operator = bell_draw(key_of[3], (NY, NY), NY ** -0.5, 0.625)
    z_operator = bell_draw(key_of[4], (NZ, NZ), NZ ** -0.5, 0.4375)
    w_in = bell_draw(key_of[5], (HIDDEN_SIZE, FEATURES), FEATURES ** -0.5, 1.25)
    b_in = bell_draw(key_of[6], (HIDDEN_SIZE,), 0.5, 3.0, (), jnp.float32)
    w_out = bell_draw(key_of[7], (FIELDS, HIDDEN_SIZE), HIDDEN_SIZE ** -0.5, 0.75)
    b_out = bell_draw(key_of[8], (FIELDS,), 0.5, 3.0, (), jnp.float32)
    return {"state": state, "cotangent": cotangent, "x_operator": x_operator, "y_operator": y_operator, "z_operator": z_operator, "w_in": w_in, "b_in": b_in, "w_out": w_out, "b_out": b_out}


STEP_SIZE = 0.5

def row_work(state_row, grad_xb, grad_yb, grad_zb, cot_row, w_in, b_in, w_out, b_out):
    fields = state_row.shape[0]
    cells = state_row.shape[1]
    features = jnp.concatenate([state_row, grad_xb, grad_yb, grad_zb], axis=0)
    before = jnp.dot(w_in, features, preferred_element_type=jnp.float32) + b_in[:, None]
    active = jnp.tanh(before)
    hidden = active.astype(jnp.bfloat16)
    closure = jnp.dot(w_out, hidden, preferred_element_type=jnp.float32) + b_out[:, None]
    state_f = state_row.astype(jnp.float32)
    grad_xf = grad_xb.astype(jnp.float32)
    grad_yf = grad_yb.astype(jnp.float32)
    grad_zf = grad_zb.astype(jnp.float32)
    vel_x = state_f[0:1]
    vel_y = state_f[1:2]
    vel_z = state_f[2:3]
    advect = vel_x * grad_xf + vel_y * grad_yf + vel_z * grad_zf
    updated = (state_f + STEP_SIZE * (closure - advect)).astype(jnp.bfloat16)
    cot_f = cot_row.astype(jnp.float32)
    d_closure = (STEP_SIZE * cot_f).astype(jnp.bfloat16)
    w_out_part = jnp.dot(d_closure, hidden.T, preferred_element_type=jnp.float32)
    b_out_part = lax.optimization_barrier(jnp.sum(d_closure.astype(jnp.float32), axis=1))
    d_hidden = jnp.dot(w_out.T, d_closure, preferred_element_type=jnp.float32)
    d_before = (d_hidden * (1.0 - active * active)).astype(jnp.bfloat16)
    w_in_part = jnp.dot(d_before, features.T, preferred_element_type=jnp.float32)
    b_in_part = lax.optimization_barrier(jnp.sum(d_before.astype(jnp.float32), axis=1))
    d_features = jnp.dot(w_in.T, d_before, preferred_element_type=jnp.float32)
    d_advect = -STEP_SIZE * cot_f
    cot_x = (d_features[fields:2 * fields] + d_advect * vel_x).astype(jnp.bfloat16)
    cot_y = (d_features[2 * fields:3 * fields] + d_advect * vel_y).astype(jnp.bfloat16)
    cot_z = (d_features[3 * fields:4 * fields] + d_advect * vel_z).astype(jnp.bfloat16)
    velocity = jnp.stack([lax.optimization_barrier(jnp.sum(d_advect * grad_xf, axis=0)), lax.optimization_barrier(jnp.sum(d_advect * grad_yf, axis=0)), lax.optimization_barrier(jnp.sum(d_advect * grad_zf, axis=0))])
    padded = jnp.concatenate([velocity, jnp.zeros((fields - 3, cells), jnp.float32)], axis=0)
    local = cot_f + d_features[0:fields] + padded
    return (updated, local, cot_x, cot_y, cot_z, w_in_part, b_in_part, w_out_part, b_out_part)

def reference(state, cotangent, x_operator, y_operator, z_operator, w_in, b_in, w_out, b_out):
    x_full = x_operator.astype(jnp.float32)
    y_full = y_operator.astype(jnp.float32)
    z_full = z_operator.astype(jnp.float32)

    def one_member(member_pair):
        state_one, cot_one = member_pair
        state_f32 = state_one.astype(jnp.float32)
        grad_x = jnp.einsum('ia,fajk->fijk', x_full, state_f32).astype(jnp.bfloat16)
        grad_y = jnp.einsum('ja,fiak->fijk', y_full, state_f32).astype(jnp.bfloat16)
        grad_z = jnp.einsum('ka,fija->fijk', z_full, state_f32).astype(jnp.bfloat16)

        def plane_work(items):
            flat = [item.reshape(FIELDS, NY * NZ) for item in items]
            return row_work(flat[0], flat[1], flat[2], flat[3], flat[4], w_in, b_in, w_out, b_out)
        planes = lax.map(plane_work, tuple((jnp.moveaxis(item, 1, 0) for item in (state_one, grad_x, grad_y, grad_z, cot_one))))

        def restore(value):
            return jnp.moveaxis(value.reshape(NX, FIELDS, NY, NZ), 0, 1)
        updated = restore(planes[0])
        local = restore(planes[1])
        cot_x = restore(planes[2]).astype(jnp.float32)
        cot_y = restore(planes[3]).astype(jnp.float32)
        cot_z = restore(planes[4]).astype(jnp.float32)
        adjoint = local + jnp.einsum('ai,fajk->fijk', x_full, cot_x)
        adjoint = adjoint + jnp.einsum('aj,fiak->fijk', y_full, cot_y)
        adjoint = adjoint + jnp.einsum('ak,fija->fijk', z_full, cot_z)
        return (updated, adjoint.astype(jnp.bfloat16), lax.optimization_barrier(jnp.sum(planes[5], axis=0)), lax.optimization_barrier(jnp.sum(planes[6], axis=0)), lax.optimization_barrier(jnp.sum(planes[7], axis=0)), lax.optimization_barrier(jnp.sum(planes[8], axis=0)))
    outcome = lax.map(one_member, (state, cotangent))
    scaling = 1.0 / math.sqrt(TRAJ * NX * NY * NZ)
    return (outcome[0], outcome[1], lax.optimization_barrier(jnp.sum(outcome[2], axis=0)) * scaling, lax.optimization_barrier(jnp.sum(outcome[3], axis=0)) * scaling, lax.optimization_barrier(jnp.sum(outcome[4], axis=0)) * scaling, lax.optimization_barrier(jnp.sum(outcome[5], axis=0)) * scaling)
```

```python
import functools
import math

import jax
import jax.numpy as jnp
from jax import lax
from jax.experimental import pallas as pl
from jax.experimental.pallas import tpu as pltpu
from jax.sharding import PartitionSpec as P

MESH = pl.DeviceIdType.MESH
F32 = jnp.float32
BF16 = jnp.bfloat16
GROUP = 16
FIELDS = 5
HIDDEN = 64
PACK = 384
WIDE = 768
CHUNKS = 3
CHANNELS = 4 * FIELDS
EXTENDED = CHANNELS + 3


def pack(a, b):
    tail = jnp.concatenate([a[..., 128:192], b[..., 128:192]], axis=-1)
    return jnp.concatenate([a[..., 0:128], b[..., 0:128], tail], axis=-1)


def unpack(p):
    a = jnp.concatenate([p[..., 0:128], p[..., 256:320]], axis=-1)
    b = jnp.concatenate([p[..., 128:256], p[..., 320:384]], axis=-1)
    return a, b


def widen(v):
    return jnp.concatenate([v[:, 0:8], v[:, 8:16]], axis=-1)


def narrow(v):
    return jnp.concatenate([v[..., 0:PACK], v[..., PACK:WIDE]], axis=1)


def dot(a, b):
    return jnp.dot(a, b, preferred_element_type=F32)


def dot_t(a, b):
    return lax.dot_general(a, b, (((1,), (1,)), ((), ())), preferred_element_type=F32)


def step_kernel(
    s_ref, c_ref, x_ref, xt_ref, y_ref, yt_ref, z_ref, zt_ref, perm_ref,
    w1_ref, w1t_ref, w2_ref, w2t_ref, bo_ref,
    ns_ref, sg_ref, g1_ref, g2_ref, g3_ref,
    send, pen, recv, gx, gy, gz, cx, cy, cz, loc, ssem, rsem, lsem,
):
    me = lax.axis_index("space")

    def copy_of(phase, c, s, target):
        dst = lax.rem(me + s, GROUP)
        return pltpu.make_async_remote_copy(
            src_ref=send.at[c, dst],
            dst_ref=target.at[c, me],
            send_sem=ssem.at[phase, c, s],
            recv_sem=rsem.at[phase, c, s],
            device_id={"space": dst},
            device_id_type=MESH,
        )

    def own_of(phase, c, target):
        return pltpu.make_async_copy(send.at[c, me], target.at[c, me], lsem.at[phase, c])

    def start(phase, c, target):
        own_of(phase, c, target).start()

        def one(s, carry):
            copy_of(phase, c, s, target).start()
            return carry

        lax.fori_loop(1, GROUP, one, 0)

    def finish(phase, c, target):
        own_of(phase, c, target).wait()

        def one(s, carry):
            copy_of(phase, c, s, target).wait()
            return carry

        lax.fori_loop(1, GROUP, one, 0)

    def rows(c, half):
        return pl.ds(pl.multiple_of(c * 32 + 16 * half, 16), 16)

    barrier = pltpu.get_barrier_semaphore()

    def greet(s, carry):
        pl.semaphore_signal(
            barrier, inc=1, device_id={"space": lax.rem(me + s, GROUP)}, device_id_type=MESH
        )
        return carry

    lax.fori_loop(1, GROUP, greet, 0)
    pl.semaphore_wait(barrier, GROUP - 1)

    def send_state(c, carry):
        for f in range(FIELDS):
            a = s_ref[f, :, rows(c, 0), :].reshape(256, 192)
            b = s_ref[f, :, rows(c, 1), :].reshape(256, 192)
            moved = dot(perm_ref[...], pack(a, b)).astype(BF16)
            send[c, :, :, f * PACK : (f + 1) * PACK] = moved.reshape(16, 16, PACK)
        start(0, c, pen)
        return carry

    lax.fori_loop(0, CHUNKS, send_state, 0)

    def lines(a, carry):
        for f in range(FIELDS):
            s = s_ref[f, a]
            dy = dot(y_ref[...], s).astype(BF16)
            dz = dot(s, zt_ref[...]).astype(BF16)
            for c in range(CHUNKS):
                lo, mid, hi = 32 * c, 32 * c + 16, 32 * c + 32
                gy[c, f, a] = pack(dy[lo:mid], dy[mid:hi])
                gz[c, f, a] = pack(dz[lo:mid], dz[mid:hi])
        return carry

    lax.fori_loop(0, GROUP, lines, 0)

    g1_ref[...] = jnp.zeros_like(g1_ref)
    g2_ref[...] = jnp.zeros_like(g2_ref)
    g3_ref[...] = jnp.zeros_like(g3_ref)

    def streamwise(c, operator):
        for f in range(FIELDS):
            lanes = slice(f * PACK, (f + 1) * PACK)
            done = dot(operator[...], pen[c, :, :, lanes].reshape(256, PACK)).astype(BF16)
            send[c, :, :, lanes] = done.reshape(16, 16, PACK)

    def forward_lines(c, carry):
        finish(0, c, pen)
        streamwise(c, x_ref)
        start(1, c, recv)
        return carry

    lax.fori_loop(0, CHUNKS, forward_lines, 0)

    def closure(c, a):
        state = pack(s_ref[:, a, rows(c, 0), :], s_ref[:, a, rows(c, 1), :])
        cot = pack(c_ref[:, a, rows(c, 0), :], c_ref[:, a, rows(c, 1), :])
        features = widen(
            jnp.concatenate([state, gx[:, a], gy[c, :, a], gz[c, :, a]], axis=0).astype(F32)
        )
        cw = widen(cot.astype(F32))
        ones = jnp.ones((3, 8, WIDE), F32)
        fb = jnp.concatenate([features, ones], axis=0).reshape(EXTENDED * 8, WIDE).astype(BF16)
        active = jnp.tanh(dot(w1_ref[...], fb))
        hidden = active.astype(BF16)
        closed = dot(w2_ref[...], hidden).reshape(FIELDS, 8, WIDE)
        half = 0.5 * cw
        d_closure = half.reshape(FIELDS * 8, WIDE).astype(BF16)
        d_hidden = dot(w2t_ref[...], d_closure)
        d_before = (d_hidden * (1.0 - active * active)).astype(BF16)
        d_features = dot(w1t_ref[...], d_before).reshape(CHANNELS, 8, WIDE)
        g1_ref[...] += dot_t(d_before, fb)
        g2_ref[...] += dot_t(hidden, d_closure)
        dc = d_closure.astype(F32)
        g3_ref[...] += sum(dc[:, 128 * t : 128 * (t + 1)] for t in range(WIDE // 128))
        u, v, w = features[0:1], features[1:2], features[2:3]
        fx, fy, fz = features[5:10], features[10:15], features[15:20]
        advect = u * fx + v * fy + w * fz
        bias = jnp.stack([jnp.full((8, WIDE), bo_ref[f], F32) for f in range(FIELDS)])
        updated = narrow(features[0:5] + 0.5 * (closed + bias - advect)).astype(BF16)
        first, second = unpack(updated)
        ns_ref[:, a, rows(c, 0), :] = first
        ns_ref[:, a, rows(c, 1), :] = second
        cx[:, a] = narrow(d_features[5:10] - half * u).astype(BF16)
        cy[c, :, a] = narrow(d_features[10:15] - half * v).astype(BF16)
        cz[c, :, a] = narrow(d_features[15:20] - half * w).astype(BF16)
        vel = [-jnp.sum(half * g, axis=0, keepdims=True) for g in (fx, fy, fz)]
        padded = jnp.concatenate(vel + [jnp.zeros((2, 8, WIDE), F32)], axis=0)
        loc[c, :, a] = narrow(cw + d_features[0:5] + padded)

    def backward_lines(c):
        finish(2, c, pen)
        streamwise(c, xt_ref)
        start(3, c, recv)

    def middle(c, carry):
        finish(1, c, recv)
        for f in range(FIELDS):
            lanes = slice(f * PACK, (f + 1) * PACK)
            back = dot(perm_ref[...], recv[c, :, :, lanes].reshape(256, PACK)).astype(BF16)
            gx[f] = back.reshape(16, 16, PACK)

        def plane(a, inner):
            closure(c, a)
            return inner

        lax.fori_loop(0, GROUP, plane, 0)
        for f in range(FIELDS):
            lanes = slice(f * PACK, (f + 1) * PACK)
            moved = dot(perm_ref[...], cx[f].reshape(256, PACK)).astype(BF16)
            send[c, :, :, lanes] = moved.reshape(16, 16, PACK)
        start(2, c, pen)

        @pl.when(c >= 1)
        def _():
            backward_lines(c - 1)

        return carry

    lax.fori_loop(0, CHUNKS, middle, 0)

    def adjoint_lines(a, carry):
        for f in range(FIELDS):
            ys, zs = [], []
            for c in range(CHUNKS):
                ys += unpack(cy[c, f, a])
                zs += unpack(cz[c, f, a])
            total = dot(yt_ref[...], jnp.concatenate(ys, axis=0))
            total += dot(jnp.concatenate(zs, axis=0), z_ref[...])
            for c in range(CHUNKS):
                lo, mid, hi = 32 * c, 32 * c + 16, 32 * c + 32
                loc[c, f, a] += pack(total[lo:mid], total[mid:hi])
        return carry

    lax.fori_loop(0, GROUP, adjoint_lines, 0)
    backward_lines(CHUNKS - 1)

    def last(c, carry):
        finish(3, c, recv)
        for f in range(FIELDS):
            lanes = slice(f * PACK, (f + 1) * PACK)
            back = dot(perm_ref[...], recv[c, :, :, lanes].reshape(256, PACK))
            whole = (back.reshape(16, 16, PACK) + loc[c, f]).astype(BF16)
            first, second = unpack(whole)
            sg_ref[f, :, rows(c, 0), :] = first
            sg_ref[f, :, rows(c, 1), :] = second
        return carry

    lax.fori_loop(0, CHUNKS, last, 0)


def spread(w):
    n, m = w.shape
    eye = jnp.eye(8, dtype=w.dtype)
    return (w[:, None, :, None] * eye[None, :, None, :]).reshape(n * 8, m * 8)


def gather(g, n, m):
    eye = jnp.eye(8, dtype=F32)
    return jnp.sum(g.reshape(n, 8, m, 8) * eye[None, :, None, :], axis=(1, 3))


def body(state, cotangent, x_operator, y_operator, z_operator, w_in, b_in, w_out, b_out):
    shape = state.shape[1:]
    hi = lax.reduce_precision(b_in, 8, 7)
    mid = lax.reduce_precision(b_in - hi, 8, 7)
    low = b_in - hi - mid
    columns = jnp.stack([hi, mid, low], axis=1).astype(BF16)
    w1 = spread(jnp.concatenate([w_in, columns], axis=1))
    w1t = spread(w_in.T)
    w2 = spread(w_out)
    w2t = spread(w_out.T)
    place = jnp.arange(256)
    swapped = (place % 16) * 16 + place // 16
    perm = (swapped[:, None] == place[None, :]).astype(BF16)
    vmem = pl.BlockSpec(memory_space=pltpu.VMEM)
    buffer = pltpu.VMEM((CHUNKS, GROUP, GROUP, FIELDS * PACK), BF16)
    packed = pltpu.VMEM((CHUNKS, FIELDS, GROUP, GROUP, PACK), BF16)
    part = pltpu.VMEM((FIELDS, GROUP, GROUP, PACK), BF16)
    ns, sg, g1, g2, g3 = pl.pallas_call(
        step_kernel,
        out_shape=(
            jax.ShapeDtypeStruct(shape, BF16),
            jax.ShapeDtypeStruct(shape, BF16),
            jax.ShapeDtypeStruct((HIDDEN * 8, EXTENDED * 8), F32),
            jax.ShapeDtypeStruct((HIDDEN * 8, FIELDS * 8), F32),
            jax.ShapeDtypeStruct((FIELDS * 8, 128), F32),
        ),
        in_specs=[vmem] * 13 + [pl.BlockSpec(memory_space=pltpu.SMEM)],
        out_specs=[vmem] * 5,
        scratch_shapes=[
            buffer, buffer, buffer, part, packed, packed, part, packed, packed,
            pltpu.VMEM((CHUNKS, FIELDS, GROUP, GROUP, PACK), F32),
            pltpu.SemaphoreType.DMA((4, CHUNKS, GROUP)),
            pltpu.SemaphoreType.DMA((4, CHUNKS, GROUP)),
            pltpu.SemaphoreType.DMA((4, CHUNKS)),
        ],
        compiler_params=pltpu.CompilerParams(
            collective_id=0, has_side_effects=True, vmem_limit_bytes=60 * 1024 * 1024
        ),
        cost_estimate=pl.CostEstimate(flops=10**11, bytes_accessed=2 * 10**7, transcendentals=2 * 10**7),
        name="evolution",
    )(
        state[0], cotangent[0], x_operator, x_operator.T, y_operator, y_operator.T,
        z_operator, z_operator.T, perm, w1, w1t, w2, w2t, b_out,
    )
    w_in_all = gather(g1, HIDDEN, EXTENDED)
    w_out_all = gather(g2, HIDDEN, FIELDS).T
    b_out_all = jnp.sum(g3.reshape(FIELDS, 8 * 128), axis=1)
    summed = lax.psum((w_in_all, w_out_all, b_out_all), ("dp", "space"))
    cells = (
        lax.axis_size("dp") * lax.axis_size("space") * shape[1] * shape[2] * shape[3]
    )
    scaling = 1.0 / math.sqrt(cells)
    return (
        ns[None],
        sg[None],
        summed[0][:, 0:CHANNELS] * scaling,
        summed[0][:, CHANNELS] * scaling,
        summed[1] * scaling,
        summed[2] * scaling,
    )


def solution(mesh):
    wide = P("dp", None, "space", None, None)
    return jax.shard_map(
        body,
        mesh=mesh,
        in_specs=(wide, wide) + (P(),) * 7,
        out_specs=(wide, wide) + (P(),) * 4,
        check_vma=False,
    )
```

```python
import functools
import math

import jax
import jax.numpy as jnp
from jax import lax
from jax.experimental import pallas as pl
from jax.experimental.pallas import tpu as pltpu
from jax.sharding import PartitionSpec as P

MESH = pl.DeviceIdType.MESH
F32 = jnp.float32
BF16 = jnp.bfloat16
GROUP = 16
FIELDS = 5
HIDDEN = 64
PACK = 384
WIDE = 768
CHUNKS = 3
CHANNELS = 4 * FIELDS
EXTENDED = CHANNELS + 3


def pack(a, b):
    tail = jnp.concatenate([a[..., 128:192], b[..., 128:192]], axis=-1)
    return jnp.concatenate([a[..., 0:128], b[..., 0:128], tail], axis=-1)


def unpack(p):
    a = jnp.concatenate([p[..., 0:128], p[..., 256:320]], axis=-1)
    b = jnp.concatenate([p[..., 128:256], p[..., 320:384]], axis=-1)
    return a, b


def widen(v):
    return jnp.concatenate([v[:, 0:8], v[:, 8:16]], axis=-1)


def narrow(v):
    return jnp.concatenate([v[..., 0:PACK], v[..., PACK:WIDE]], axis=1)


def dot(a, b):
    return jnp.dot(a, b, preferred_element_type=F32)


def dot_t(a, b):
    return lax.dot_general(a, b, (((1,), (1,)), ((), ())), preferred_element_type=F32)


def iota(shape, axis):
    return lax.broadcasted_iota(jnp.int32, shape, axis)


def where_equal(shape, left, right):
    return jnp.where(left(iota(shape, 0)) == right(iota(shape, 1)), 1.0, 0.0)


def same(i):
    return i


def eighth(i):
    return i // 8


def step_kernel(
    s_hbm, c_hbm, x_ref, y_ref, z_ref, wi_ref, wit_ref, b_ref, wo_ref, wot_ref, bo_ref,
    ns_hbm, sg_hbm, total_ref,
    s_ref, c_ref, ns_ref, xt_ref, yt_ref, zt_ref, perm_ref, w1_ref, w1t_ref, w2_ref, w2t_ref,
    g1_ref, g2_ref, g3_ref, pay, slots, piece, ssem, rsem, lsem, msem, nsem, iosem,
    send, pen, recv, gx, gy, gz, cx, cy, cz, loc,
):
    me = lax.axis_index("space")
    team = lax.axis_index("dp")

    def copy_of(phase, c, s, target):
        dst = lax.rem(me + s, GROUP)
        return pltpu.make_async_remote_copy(
            src_ref=send.at[c, dst],
            dst_ref=target.at[c, me],
            send_sem=ssem.at[phase, c, s],
            recv_sem=rsem.at[phase, c, s],
            device_id={"space": dst},
            device_id_type=MESH,
        )

    def own_of(phase, c, target):
        return pltpu.make_async_copy(send.at[c, me], target.at[c, me], lsem.at[phase, c])

    def each(one):
        def run(s, carry):
            one(s)
            return carry

        lax.fori_loop(1, GROUP, run, 0)

    def start(phase, c, target):
        own_of(phase, c, target).start()
        each(lambda s: copy_of(phase, c, s, target).start())

    def finish(phase, c, target):
        own_of(phase, c, target).wait()
        each(lambda s: copy_of(phase, c, s, target).wait())

    def rows(c, half):
        return pl.ds(pl.multiple_of(c * 32 + 16 * half, 16), 16)

    def chunk(c):
        return pl.ds(pl.multiple_of(c * 32, 32), 32)

    def load_state(c):
        return pltpu.make_async_copy(
            s_hbm.at[:, :, chunk(c), :], s_ref.at[:, :, chunk(c), :], iosem.at[0, c]
        )

    def load_cotangent(c):
        return pltpu.make_async_copy(
            c_hbm.at[:, :, chunk(c), :], c_ref.at[:, :, chunk(c), :], iosem.at[1, c]
        )

    def store_state(c):
        return pltpu.make_async_copy(
            ns_ref.at[:, :, chunk(c), :], ns_hbm.at[:, :, chunk(c), :], iosem.at[2, c]
        )

    def store_grad(c):
        return pltpu.make_async_copy(
            s_ref.at[:, :, chunk(c), :], sg_hbm.at[:, :, chunk(c), :], iosem.at[3, c]
        )

    for c in range(CHUNKS):
        load_state(c).start()
    for c in range(CHUNKS):
        load_cotangent(c).start()

    barrier = pltpu.get_barrier_semaphore()
    for axis, mine in (("space", me), ("dp", team)):

        def greet(s, axis=axis, mine=mine):
            pl.semaphore_signal(
                barrier, inc=1, device_id={axis: lax.rem(mine + s, GROUP)}, device_id_type=MESH
            )

        each(greet)
    perm_ref[...] = where_equal(
        (256, 256), lambda i: (i % 16) * 16 + i // 16, same
    ).astype(BF16)
    pl.semaphore_wait(barrier, 2 * (GROUP - 1))

    def send_state(c, carry):
        load_state(c).wait()
        for f in range(FIELDS):
            a = s_ref[f, :, rows(c, 0), :].reshape(256, 192)
            b = s_ref[f, :, rows(c, 1), :].reshape(256, 192)
            moved = dot(perm_ref[...], pack(a, b)).astype(BF16)
            send[c, :, :, f * PACK : (f + 1) * PACK] = moved.reshape(16, 16, PACK)
        start(0, c, pen)
        return carry

    lax.fori_loop(0, CHUNKS, send_state, 0)

    for source, target in ((x_ref, xt_ref), (y_ref, yt_ref), (z_ref, zt_ref)):
        unit = where_equal(source.shape, same, same).astype(BF16)
        target[...] = dot_t(unit, source[...]).astype(BF16)

    def spread(w):
        n, m = w.shape
        left = where_equal((n * 8, n), eighth, same).astype(BF16)
        right = where_equal((m, m * 8), same, eighth).astype(BF16)
        return dot(left, dot(w, right).astype(BF16)) * diagonal((n * 8, m * 8))

    def diagonal(shape):
        return where_equal(shape, lambda i: i % 8, lambda i: i % 8)

    bias = b_ref[...]
    high = bias.astype(BF16).astype(F32)
    mid = (bias - high).astype(BF16).astype(F32)
    low = bias - high - mid
    places = iota((HIDDEN, EXTENDED * 8), 1) // 8
    right = where_equal((CHANNELS, EXTENDED * 8), same, eighth).astype(BF16)
    inner = dot(wi_ref[...], right)
    for place, column in enumerate((high, mid, low)):
        inner += jnp.where(places == CHANNELS + place, column, 0.0)
    left = where_equal((HIDDEN * 8, HIDDEN), eighth, same).astype(BF16)
    w1 = dot(left, inner.astype(BF16)) * diagonal((HIDDEN * 8, EXTENDED * 8))
    w1_ref[...] = w1.astype(BF16)
    w1t_ref[...] = spread(wit_ref[...]).astype(BF16)
    w2_ref[...] = spread(wo_ref[...]).astype(BF16)
    w2t_ref[...] = spread(wot_ref[...]).astype(BF16)

    def lines(a, carry):
        for f in range(FIELDS):
            s = s_ref[f, a]
            dy = dot(y_ref[...], s).astype(BF16)
            dz = dot(s, zt_ref[...]).astype(BF16)
            for c in range(CHUNKS):
                lo, mid, hi = 32 * c, 32 * c + 16, 32 * c + 32
                gy[c, f, a] = pack(dy[lo:mid], dy[mid:hi])
                gz[c, f, a] = pack(dz[lo:mid], dz[mid:hi])
        return carry

    lax.fori_loop(0, GROUP, lines, 0)

    g1_ref[...] = jnp.zeros_like(g1_ref)
    g2_ref[...] = jnp.zeros_like(g2_ref)
    g3_ref[...] = jnp.zeros_like(g3_ref)

    def streamwise(c, operator):
        for f in range(FIELDS):
            lanes = slice(f * PACK, (f + 1) * PACK)
            done = dot(operator[...], pen[c, :, :, lanes].reshape(256, PACK)).astype(BF16)
            send[c, :, :, lanes] = done.reshape(16, 16, PACK)

    def forward_lines(c, carry):
        finish(0, c, pen)
        streamwise(c, x_ref)
        start(1, c, recv)
        return carry

    lax.fori_loop(0, CHUNKS, forward_lines, 0)

    def closure(c, a):
        state = pack(s_ref[:, a, rows(c, 0), :], s_ref[:, a, rows(c, 1), :])
        cot = pack(c_ref[:, a, rows(c, 0), :], c_ref[:, a, rows(c, 1), :])
        features = widen(
            jnp.concatenate([state, gx[:, a], gy[c, :, a], gz[c, :, a]], axis=0).astype(F32)
        )
        cw = widen(cot.astype(F32))
        ones = jnp.ones((3, 8, WIDE), F32)
        fb = jnp.concatenate([features, ones], axis=0).reshape(EXTENDED * 8, WIDE).astype(BF16)
        active = jnp.tanh(dot(w1_ref[...], fb))
        hidden = active.astype(BF16)
        closed = dot(w2_ref[...], hidden).reshape(FIELDS, 8, WIDE)
        half = 0.5 * cw
        d_closure = half.reshape(FIELDS * 8, WIDE).astype(BF16)
        d_hidden = dot(w2t_ref[...], d_closure)
        d_before = (d_hidden * (1.0 - active * active)).astype(BF16)
        d_features = dot(w1t_ref[...], d_before).reshape(CHANNELS, 8, WIDE)
        g1_ref[...] += dot_t(d_before, fb)
        g2_ref[...] += dot_t(hidden, d_closure)
        dc = d_closure.astype(F32)
        g3_ref[...] += sum(dc[:, 128 * t : 128 * (t + 1)] for t in range(WIDE // 128))
        u, v, w = features[0:1], features[1:2], features[2:3]
        fx, fy, fz = features[5:10], features[10:15], features[15:20]
        advect = u * fx + v * fy + w * fz
        bias = jnp.stack([jnp.full((8, WIDE), bo_ref[f], F32) for f in range(FIELDS)])
        updated = narrow(features[0:5] + 0.5 * (closed + bias - advect)).astype(BF16)
        first, second = unpack(updated)
        ns_ref[:, a, rows(c, 0), :] = first
        ns_ref[:, a, rows(c, 1), :] = second
        cx[:, a] = narrow(d_features[5:10] - half * u).astype(BF16)
        cy[c, :, a] = narrow(d_features[10:15] - half * v).astype(BF16)
        cz[c, :, a] = narrow(d_features[15:20] - half * w).astype(BF16)
        vel = [-jnp.sum(half * g, axis=0, keepdims=True) for g in (fx, fy, fz)]
        padded = jnp.concatenate(vel + [jnp.zeros((2, 8, WIDE), F32)], axis=0)
        loc[c, :, a] = narrow(cw + d_features[0:5] + padded)

    def backward_lines(c):
        finish(2, c, pen)
        streamwise(c, xt_ref)
        start(3, c, recv)

    def middle(c, carry):
        finish(1, c, recv)
        load_cotangent(c).wait()
        for f in range(FIELDS):
            lanes = slice(f * PACK, (f + 1) * PACK)
            back = dot(perm_ref[...], recv[c, :, :, lanes].reshape(256, PACK)).astype(BF16)
            gx[f] = back.reshape(16, 16, PACK)

        def plane(a, inner):
            closure(c, a)
            return inner

        lax.fori_loop(0, GROUP, plane, 0)
        for f in range(FIELDS):
            lanes = slice(f * PACK, (f + 1) * PACK)
            moved = dot(perm_ref[...], cx[f].reshape(256, PACK)).astype(BF16)
            send[c, :, :, lanes] = moved.reshape(16, 16, PACK)
        start(2, c, pen)
        store_state(c).start()

        @pl.when(c >= 1)
        def _():
            backward_lines(c - 1)

        return carry

    lax.fori_loop(0, CHUNKS, middle, 0)

    def folded(g):
        n, m = g.shape
        return jnp.sum((g[...] * diagonal((n, m))).reshape(n // 8, 8, m), axis=1)

    def lanes_of(m, first):
        return where_equal((m, 128), lambda i: i // 8 + first, same)

    def exact(a, b):
        return jnp.dot(a, b, precision=lax.Precision.HIGHEST, preferred_element_type=F32)

    pay[...] = jnp.zeros_like(pay)
    pay[0:HIDDEN] = exact(folded(g1_ref), lanes_of(EXTENDED * 8, 0)) + exact(
        folded(g2_ref), lanes_of(FIELDS * 8, 32)
    )
    out_bias = jnp.sum(g3_ref[...].reshape(FIELDS, 8, 128), axis=1)
    pay[HIDDEN : HIDDEN + 8] = jnp.concatenate([out_bias, jnp.zeros((3, 128), F32)], axis=0)

    def eight(d):
        return pl.ds(pl.multiple_of(8 * d, 8), 8)

    def small(stage, s):
        axis, mine = (("space", me), ("dp", team), ("space", me))[stage]
        dst = lax.rem(mine + s, GROUP)
        source = pay.at[eight(dst)] if stage == 0 else piece.at[stage - 1]
        return pltpu.make_async_remote_copy(
            src_ref=source,
            dst_ref=slots.at[stage, mine],
            send_sem=msem.at[stage, s],
            recv_sem=nsem.at[stage, s],
            device_id={axis: dst},
            device_id_type=MESH,
        )

    def begin(stage):
        each(lambda s: small(stage, s).start())

    def collect(stage):
        each(lambda s: small(stage, s).wait())
        return sum(slots[stage, d] for d in range(1, GROUP)) + slots[stage, 0]

    slots[0, me] = pay[eight(me)]
    begin(0)

    def adjoint_lines(a, carry):
        for f in range(FIELDS):
            ys, zs = [], []
            for c in range(CHUNKS):
                ys += unpack(cy[c, f, a])
                zs += unpack(cz[c, f, a])
            total = dot(yt_ref[...], jnp.concatenate(ys, axis=0))
            total += dot(jnp.concatenate(zs, axis=0), z_ref[...])
            for c in range(CHUNKS):
                lo, mid, hi = 32 * c, 32 * c + 16, 32 * c + 32
                loc[c, f, a] += pack(total[lo:mid], total[mid:hi])
        return carry

    lax.fori_loop(0, GROUP, adjoint_lines, 0)
    over_space = collect(0)
    piece[0] = over_space
    slots[1, team] = over_space
    begin(1)
    backward_lines(CHUNKS - 1)
    over_all = collect(1)
    piece[1] = over_all
    slots[2, me] = over_all
    begin(2)

    def last(c, carry):
        finish(3, c, recv)
        for f in range(FIELDS):
            lanes = slice(f * PACK, (f + 1) * PACK)
            back = dot(perm_ref[...], recv[c, :, :, lanes].reshape(256, PACK))
            whole = (back.reshape(16, 16, PACK) + loc[c, f]).astype(BF16)
            first, second = unpack(whole)
            s_ref[f, :, rows(c, 0), :] = first
            s_ref[f, :, rows(c, 1), :] = second
        store_grad(c).start()
        return carry

    lax.fori_loop(0, CHUNKS - 1, last, 0)
    each(lambda s: small(2, s).wait())
    for d in range(HIDDEN // 8 + 1):
        total_ref[8 * d : 8 * d + 8] = slots[2, d]
    last(CHUNKS - 1, 0)
    for c in range(CHUNKS):
        store_state(c).wait()
    for c in range(CHUNKS):
        store_grad(c).wait()


def body(state, cotangent, x_operator, y_operator, z_operator, w_in, b_in, w_out, b_out):
    shape = state.shape[1:]
    vmem = pl.BlockSpec(memory_space=pltpu.VMEM)
    hbm = pl.BlockSpec(memory_space=pl.ANY)
    buffer = pltpu.VMEM((CHUNKS, GROUP, GROUP, FIELDS * PACK), BF16)
    packed = pltpu.VMEM((CHUNKS, FIELDS, GROUP, GROUP, PACK), BF16)
    part = pltpu.VMEM((FIELDS, GROUP, GROUP, PACK), BF16)
    whole = pltpu.VMEM(shape, BF16)
    dma = pltpu.SemaphoreType.DMA
    ns, sg, total = pl.pallas_call(
        step_kernel,
        out_shape=(
            jax.ShapeDtypeStruct(shape, BF16),
            jax.ShapeDtypeStruct(shape, BF16),
            jax.ShapeDtypeStruct((HIDDEN + 8, 128), F32),
        ),
        in_specs=[hbm] * 2 + [vmem] * 8 + [pl.BlockSpec(memory_space=pltpu.SMEM)],
        out_specs=[hbm, hbm, vmem],
        scratch_shapes=[
            whole, whole, whole,
            pltpu.VMEM(x_operator.shape, BF16),
            pltpu.VMEM(y_operator.shape, BF16),
            pltpu.VMEM(z_operator.shape, BF16),
            pltpu.VMEM((256, 256), BF16),
            pltpu.VMEM((HIDDEN * 8, EXTENDED * 8), BF16),
            pltpu.VMEM((CHANNELS * 8, HIDDEN * 8), BF16),
            pltpu.VMEM((FIELDS * 8, HIDDEN * 8), BF16),
            pltpu.VMEM((HIDDEN * 8, FIELDS * 8), BF16),
            pltpu.VMEM((HIDDEN * 8, EXTENDED * 8), F32),
            pltpu.VMEM((HIDDEN * 8, FIELDS * 8), F32),
            pltpu.VMEM((FIELDS * 8, 128), F32),
            pltpu.VMEM((128, 128), F32),
            pltpu.VMEM((3, GROUP, 8, 128), F32),
            pltpu.VMEM((2, 8, 128), F32),
            dma((4, CHUNKS, GROUP)),
            dma((4, CHUNKS, GROUP)),
            dma((4, CHUNKS)),
            dma((3, GROUP)),
            dma((3, GROUP)),
            dma((4, CHUNKS)),
            buffer, buffer, buffer, part, packed, packed, part, packed, packed,
            pltpu.VMEM((CHUNKS, FIELDS, GROUP, GROUP, PACK), F32),
        ],
        compiler_params=pltpu.CompilerParams(
            collective_id=0, has_side_effects=True, vmem_limit_bytes=60 * 1024 * 1024
        ),
        cost_estimate=pl.CostEstimate(
            flops=10**11, bytes_accessed=2 * 10**7, transcendentals=2 * 10**7
        ),
        name="evolution",
    )(
        state[0], cotangent[0], x_operator, y_operator, z_operator,
        w_in, w_in.T, b_in[:, None], w_out, w_out.T, b_out,
    )
    cells = (
        lax.axis_size("dp") * lax.axis_size("space") * shape[1] * shape[2] * shape[3]
    )
    scaled = total * (1.0 / math.sqrt(cells))
    return (
        ns[None],
        sg[None],
        scaled[0:HIDDEN, 0:CHANNELS],
        scaled[0:HIDDEN, CHANNELS],
        scaled[0:HIDDEN, 32 : 32 + FIELDS].T,
        jnp.sum(scaled[HIDDEN : HIDDEN + FIELDS], axis=1),
    )


def solution(mesh):
    wide = P("dp", None, "space", None, None)
    return jax.shard_map(
        body,
        mesh=mesh,
        in_specs=(wide, wide) + (P(),) * 7,
        out_specs=(wide, wide) + (P(),) * 4,
        check_vma=False,
    )
```

```python
import functools
import math

import jax
import jax.numpy as jnp
from jax import lax
from jax.experimental import pallas as pl
from jax.experimental.pallas import tpu as pltpu
from jax.sharding import PartitionSpec as P

MESH = pl.DeviceIdType.MESH
F32 = jnp.float32
BF16 = jnp.bfloat16
GROUP = 16
FIELDS = 5
HIDDEN = 64
PACK = 384
WIDE = 768
CHUNKS = 3
CHANNELS = 4 * FIELDS
EXTENDED = CHANNELS + 3


def pack(a, b):
    tail = jnp.concatenate([a[..., 128:192], b[..., 128:192]], axis=-1)
    return jnp.concatenate([a[..., 0:128], b[..., 0:128], tail], axis=-1)


def unpack(p):
    a = jnp.concatenate([p[..., 0:128], p[..., 256:320]], axis=-1)
    b = jnp.concatenate([p[..., 128:256], p[..., 320:384]], axis=-1)
    return a, b


def widen(v):
    return jnp.concatenate([v[:, 0:8], v[:, 8:16]], axis=-1)


def narrow(v):
    return jnp.concatenate([v[..., 0:PACK], v[..., PACK:WIDE]], axis=1)


def dot(a, b):
    return jnp.dot(a, b, preferred_element_type=F32)


def dot_t(a, b):
    return lax.dot_general(a, b, (((1,), (1,)), ((), ())), preferred_element_type=F32)


def iota(shape, axis):
    return lax.broadcasted_iota(jnp.int32, shape, axis)


def where_equal(shape, left, right):
    return jnp.where(left(iota(shape, 0)) == right(iota(shape, 1)), 1.0, 0.0)


def same(i):
    return i


def eighth(i):
    return i // 8


def step_kernel(
    scaling, s_hbm, c_hbm, x_ref, y_ref, z_ref, wit_ref, b_ref, wo_ref, bo_ref,
    ns_ref, sg_ref, total_ref,
    s_ref, c_ref, xt_ref, yt_ref, zt_ref, perm_ref, w1_ref, w1t_ref, w2_ref, w2t_ref,
    g1_ref, g2_ref, g3_ref, pay, slots, piece, ssem, rsem, lsem, msem, nsem, iosem,
    send, pen, recv, gx, gy, gz, cx, cy, cz, loc,
):
    me = lax.axis_index("space")
    team = lax.axis_index("dp")

    def shifted(s):
        return lax.rem(me // 4 + s % 4, 4) * 4 + lax.rem(me % 4 + s // 4, 4)

    def copy_of(phase, c, s, target):
        dst = shifted(s)
        return pltpu.make_async_remote_copy(
            src_ref=send.at[c, dst],
            dst_ref=target.at[c, me],
            send_sem=ssem.at[phase, c, s],
            recv_sem=rsem.at[phase, c, s],
            device_id={"space": dst},
            device_id_type=MESH,
        )

    def own_of(phase, c, target):
        return pltpu.make_async_copy(send.at[c, me], target.at[c, me], lsem.at[phase, c])

    def each(one):
        def run(s, carry):
            one(s)
            return carry

        lax.fori_loop(1, GROUP, run, 0)

    def start(phase, c, target):
        own_of(phase, c, target).start()
        each(lambda s: copy_of(phase, c, s, target).start())

    def finish(phase, c, target):
        own_of(phase, c, target).wait()
        each(lambda s: copy_of(phase, c, s, target).wait())

    def rows(c, half):
        return pl.ds(pl.multiple_of(c * 32 + 16 * half, 16), 16)

    def chunk(c):
        return pl.ds(pl.multiple_of(c * 32, 32), 32)

    def load_state(c):
        return pltpu.make_async_copy(
            s_hbm.at[:, :, chunk(c), :], s_ref.at[:, :, chunk(c), :], iosem.at[0, c]
        )

    def load_cotangent(c):
        return pltpu.make_async_copy(
            c_hbm.at[:, :, chunk(c), :], c_ref.at[:, :, chunk(c), :], iosem.at[1, c]
        )

    for c in range(CHUNKS):
        load_state(c).start()
    barrier = pltpu.get_barrier_semaphore()
    for axis, mine in (("space", me), ("dp", team)):

        def greet(s, axis=axis, mine=mine):
            pl.semaphore_signal(
                barrier, inc=1, device_id={axis: lax.rem(mine + s, GROUP)}, device_id_type=MESH
            )

        each(greet)
    perm_ref[...] = where_equal(
        (256, 256), lambda i: (i % 16) * 16 + i // 16, same
    ).astype(BF16)
    pl.semaphore_wait(barrier, 2 * (GROUP - 1))

    def send_state(c, carry):
        load_state(c).wait()
        for f in range(FIELDS):
            a = s_ref[f, :, rows(c, 0), :].reshape(256, 192)
            b = s_ref[f, :, rows(c, 1), :].reshape(256, 192)
            moved = dot(perm_ref[...], pack(a, b)).astype(BF16)
            send[c, :, :, f * PACK : (f + 1) * PACK] = moved.reshape(16, 16, PACK)
        start(0, c, pen)
        return carry

    lax.fori_loop(0, CHUNKS, send_state, 0)
    for c in range(CHUNKS):
        load_cotangent(c).start()

    for source, target in ((x_ref, xt_ref), (y_ref, yt_ref), (z_ref, zt_ref)):
        unit = where_equal(source.shape, same, same).astype(BF16)
        target[...] = dot_t(unit, source[...]).astype(BF16)

    def spread(w):
        n, m = w.shape
        left = where_equal((n * 8, n), eighth, same).astype(BF16)
        right = where_equal((m, m * 8), same, eighth).astype(BF16)
        return dot(left, dot(w, right).astype(BF16)) * diagonal((n * 8, m * 8))

    def diagonal(shape):
        return where_equal(shape, lambda i: i % 8, lambda i: i % 8)

    def turned(w):
        unit = where_equal((w.shape[1], w.shape[1]), same, same).astype(BF16)
        return dot_t(unit, w).astype(BF16)

    unit = where_equal((HIDDEN, HIDDEN), same, same)
    bias = jnp.sum(unit * b_ref[...], axis=1, keepdims=True)
    high = bias.astype(BF16).astype(F32)
    mid = (bias - high).astype(BF16).astype(F32)
    low = bias - high - mid
    places = iota((HIDDEN, EXTENDED * 8), 1) // 8
    right = where_equal((CHANNELS, EXTENDED * 8), same, eighth).astype(BF16)
    inner = dot(turned(wit_ref[...]), right)
    for place, column in enumerate((high, mid, low)):
        inner += jnp.where(places == CHANNELS + place, column, 0.0)
    left = where_equal((HIDDEN * 8, HIDDEN), eighth, same).astype(BF16)
    w1 = dot(left, inner.astype(BF16)) * diagonal((HIDDEN * 8, EXTENDED * 8))
    w1_ref[...] = w1.astype(BF16)
    w1t_ref[...] = spread(wit_ref[...]).astype(BF16)
    w2_ref[...] = spread(wo_ref[...]).astype(BF16)
    w2t_ref[...] = spread(turned(wo_ref[...])).astype(BF16)

    def lines(a, carry):
        for f in range(FIELDS):
            s = s_ref[f, a]
            dy = dot(y_ref[...], s).astype(BF16)
            dz = dot(s, zt_ref[...]).astype(BF16)
            for c in range(CHUNKS):
                lo, mid, hi = 32 * c, 32 * c + 16, 32 * c + 32
                gy[c, f, a] = pack(dy[lo:mid], dy[mid:hi])
                gz[c, f, a] = pack(dz[lo:mid], dz[mid:hi])
        return carry

    lax.fori_loop(0, GROUP, lines, 0)

    g1_ref[...] = jnp.zeros_like(g1_ref)
    g2_ref[...] = jnp.zeros_like(g2_ref)
    g3_ref[...] = jnp.zeros_like(g3_ref)

    def streamwise(c, operator):
        for f in range(FIELDS):
            lanes = slice(f * PACK, (f + 1) * PACK)
            done = dot(operator[...], pen[c, :, :, lanes].reshape(256, PACK)).astype(BF16)
            send[c, :, :, lanes] = done.reshape(16, 16, PACK)

    def forward_lines(c, carry):
        finish(0, c, pen)
        streamwise(c, x_ref)
        start(1, c, recv)
        return carry

    lax.fori_loop(0, CHUNKS, forward_lines, 0)

    def closure(c, a):
        state = pack(s_ref[:, a, rows(c, 0), :], s_ref[:, a, rows(c, 1), :])
        cot = pack(c_ref[:, a, rows(c, 0), :], c_ref[:, a, rows(c, 1), :])
        features = widen(
            jnp.concatenate([state, gx[:, a], gy[c, :, a], gz[c, :, a]], axis=0).astype(F32)
        )
        cw = widen(cot.astype(F32))
        ones = jnp.ones((3, 8, WIDE), F32)
        fb = jnp.concatenate([features, ones], axis=0).reshape(EXTENDED * 8, WIDE).astype(BF16)
        active = jnp.tanh(dot(w1_ref[...], fb))
        hidden = active.astype(BF16)
        closed = dot(w2_ref[...], hidden).reshape(FIELDS, 8, WIDE)
        half = 0.5 * cw
        d_closure = half.reshape(FIELDS * 8, WIDE).astype(BF16)
        d_hidden = dot(w2t_ref[...], d_closure)
        d_before = (d_hidden * (1.0 - active * active)).astype(BF16)
        d_features = dot(w1t_ref[...], d_before).reshape(CHANNELS, 8, WIDE)
        g1_ref[...] += dot_t(d_before, fb)
        g2_ref[...] += dot_t(hidden, d_closure)
        dc = d_closure.astype(F32)
        g3_ref[...] += sum(dc[:, 128 * t : 128 * (t + 1)] for t in range(WIDE // 128))
        u, v, w = features[0:1], features[1:2], features[2:3]
        fx, fy, fz = features[5:10], features[10:15], features[15:20]
        advect = u * fx + v * fy + w * fz
        bias = jnp.stack([jnp.full((8, WIDE), bo_ref[f], F32) for f in range(FIELDS)])
        updated = narrow(features[0:5] + 0.5 * (closed + bias - advect)).astype(BF16)
        first, second = unpack(updated)
        ns_ref[:, a, rows(c, 0), :] = first
        ns_ref[:, a, rows(c, 1), :] = second
        cx[:, a] = narrow(d_features[5:10] - half * u).astype(BF16)
        cy[c, :, a] = narrow(d_features[10:15] - half * v).astype(BF16)
        cz[c, :, a] = narrow(d_features[15:20] - half * w).astype(BF16)
        vel = [-jnp.sum(half * g, axis=0, keepdims=True) for g in (fx, fy, fz)]
        padded = jnp.concatenate(vel + [jnp.zeros((2, 8, WIDE), F32)], axis=0)
        loc[c, :, a] = narrow(cw + d_features[0:5] + padded)

    def backward_lines(c):
        finish(2, c, pen)
        streamwise(c, xt_ref)
        start(3, c, recv)

    def middle(c, carry):
        finish(1, c, recv)
        load_cotangent(c).wait()
        for f in range(FIELDS):
            lanes = slice(f * PACK, (f + 1) * PACK)
            back = dot(perm_ref[...], recv[c, :, :, lanes].reshape(256, PACK)).astype(BF16)
            gx[f] = back.reshape(16, 16, PACK)

        def plane(a, inner):
            closure(c, a)
            return inner

        lax.fori_loop(0, GROUP, plane, 0)
        for f in range(FIELDS):
            lanes = slice(f * PACK, (f + 1) * PACK)
            moved = dot(perm_ref[...], cx[f].reshape(256, PACK)).astype(BF16)
            send[c, :, :, lanes] = moved.reshape(16, 16, PACK)
        start(2, c, pen)

        @pl.when(c >= 1)
        def _():
            backward_lines(c - 1)

        return carry

    lax.fori_loop(0, CHUNKS, middle, 0)

    def folded(g):
        n, m = g.shape
        return jnp.sum((g[...] * diagonal((n, m))).reshape(n // 8, 8, m), axis=1)

    def summed(g, first):
        select = where_equal((40, g.shape[1]), same, lambda i: i // 8 + first)
        return lax.dot_general(
            select, folded(g), (((1,), (1,)), ((), ())),
            precision=lax.Precision.HIGHEST, preferred_element_type=F32,
        )

    pay[...] = jnp.zeros_like(pay)
    pay[0:40, 0:HIDDEN] = summed(g1_ref, 0) + summed(g2_ref, 32)
    out_bias = jnp.sum(g3_ref[...].reshape(FIELDS, 8, 128), axis=1)
    pay[40:48] = jnp.concatenate([out_bias, jnp.zeros((3, 128), F32)], axis=0)

    def eight(d):
        return pl.ds(pl.multiple_of(8 * d, 8), 8)

    def small(stage, s):
        axis, mine = (("space", me), ("dp", team), ("space", me))[stage]
        dst = lax.rem(mine + s, GROUP)
        source = pay.at[eight(dst)] if stage == 0 else piece.at[stage - 1]
        return pltpu.make_async_remote_copy(
            src_ref=source,
            dst_ref=slots.at[stage, mine],
            send_sem=msem.at[stage, s],
            recv_sem=nsem.at[stage, s],
            device_id={axis: dst},
            device_id_type=MESH,
        )

    def begin(stage):
        each(lambda s: small(stage, s).start())

    def collect(stage):
        each(lambda s: small(stage, s).wait())
        return sum(slots[stage, d] for d in range(1, GROUP)) + slots[stage, 0]

    slots[0, me] = pay[eight(me)]
    begin(0)

    def adjoint_lines(a, carry):
        for f in range(FIELDS):
            ys, zs = [], []
            for c in range(CHUNKS):
                ys += unpack(cy[c, f, a])
                zs += unpack(cz[c, f, a])
            total = dot(yt_ref[...], jnp.concatenate(ys, axis=0))
            total += dot(jnp.concatenate(zs, axis=0), z_ref[...])
            for c in range(CHUNKS):
                lo, mid, hi = 32 * c, 32 * c + 16, 32 * c + 32
                loc[c, f, a] += pack(total[lo:mid], total[mid:hi])
        return carry

    lax.fori_loop(0, GROUP, adjoint_lines, 0)
    over_space = collect(0)
    piece[0] = over_space
    slots[1, team] = over_space
    begin(1)
    backward_lines(CHUNKS - 1)
    over_all = collect(1) * scaling
    piece[1] = over_all
    slots[2, me] = over_all
    begin(2)

    def last(c, carry):
        finish(3, c, recv)
        for f in range(FIELDS):
            lanes = slice(f * PACK, (f + 1) * PACK)
            back = dot(perm_ref[...], recv[c, :, :, lanes].reshape(256, PACK))
            whole = (back.reshape(16, 16, PACK) + loc[c, f]).astype(BF16)
            first, second = unpack(whole)
            sg_ref[f, :, rows(c, 0), :] = first
            sg_ref[f, :, rows(c, 1), :] = second
        return carry

    lax.fori_loop(0, CHUNKS - 1, last, 0)
    each(lambda s: small(2, s).wait())
    for d in range(6):
        total_ref[8 * d : 8 * d + 8] = slots[2, d]
    last(CHUNKS - 1, 0)


def body(state, cotangent, x_operator, y_operator, z_operator, w_in, b_in, w_out, b_out):
    shape = state.shape[1:]
    vmem = pl.BlockSpec(memory_space=pltpu.VMEM)
    hbm = pl.BlockSpec(memory_space=pl.ANY)
    buffer = pltpu.VMEM((CHUNKS, GROUP, GROUP, FIELDS * PACK), BF16)
    packed = pltpu.VMEM((CHUNKS, FIELDS, GROUP, GROUP, PACK), BF16)
    part = pltpu.VMEM((FIELDS, GROUP, GROUP, PACK), BF16)
    whole = pltpu.VMEM(shape, BF16)
    dma = pltpu.SemaphoreType.DMA
    cells = (
        lax.axis_size("dp") * lax.axis_size("space") * shape[1] * shape[2] * shape[3]
    )
    ns, sg, total = pl.pallas_call(
        functools.partial(step_kernel, 1.0 / math.sqrt(cells)),
        out_shape=(
            pltpu.VMEM(shape, BF16),
            pltpu.VMEM(shape, BF16),
            jax.ShapeDtypeStruct((48, 128), F32),
        ),
        in_specs=[hbm] * 2 + [vmem] * 6 + [pl.BlockSpec(memory_space=pltpu.SMEM)],
        out_specs=[vmem] * 3,
        scratch_shapes=[
            whole, whole,
            pltpu.VMEM(x_operator.shape, BF16),
            pltpu.VMEM(y_operator.shape, BF16),
            pltpu.VMEM(z_operator.shape, BF16),
            pltpu.VMEM((256, 256), BF16),
            pltpu.VMEM((HIDDEN * 8, EXTENDED * 8), BF16),
            pltpu.VMEM((CHANNELS * 8, HIDDEN * 8), BF16),
            pltpu.VMEM((FIELDS * 8, HIDDEN * 8), BF16),
            pltpu.VMEM((HIDDEN * 8, FIELDS * 8), BF16),
            pltpu.VMEM((HIDDEN * 8, EXTENDED * 8), F32),
            pltpu.VMEM((HIDDEN * 8, FIELDS * 8), F32),
            pltpu.VMEM((FIELDS * 8, 128), F32),
            pltpu.VMEM((128, 128), F32),
            pltpu.VMEM((3, GROUP, 8, 128), F32),
            pltpu.VMEM((2, 8, 128), F32),
            dma((4, CHUNKS, GROUP)),
            dma((4, CHUNKS, GROUP)),
            dma((4, CHUNKS)),
            dma((3, GROUP)),
            dma((3, GROUP)),
            dma((2, CHUNKS)),
            buffer, buffer, buffer, part, packed, packed, part, packed, packed,
            pltpu.VMEM((CHUNKS, FIELDS, GROUP, GROUP, PACK), F32),
        ],
        compiler_params=pltpu.CompilerParams(
            collective_id=0, has_side_effects=True, vmem_limit_bytes=52 * 1024 * 1024
        ),
        cost_estimate=pl.CostEstimate(
            flops=10**11, bytes_accessed=2 * 10**7, transcendentals=2 * 10**7
        ),
        name="evolution",
    )(
        state[0], cotangent[0], x_operator, y_operator, z_operator,
        w_in.T, b_in[None, :], w_out, b_out,
    )
    return (
        ns[None],
        sg[None],
        total[0:CHANNELS, 0:HIDDEN].T,
        total[CHANNELS, 0:HIDDEN],
        total[32 : 32 + FIELDS, 0:HIDDEN],
        jnp.sum(total[40 : 40 + FIELDS], axis=1),
    )


def solution(mesh):
    wide = P("dp", None, "space", None, None)
    return jax.shard_map(
        body,
        mesh=mesh,
        in_specs=(wide, wide) + (P(),) * 7,
        out_specs=(wide, wide) + (P(),) * 4,
        check_vma=False,
    )
```

```python
import functools
import math

import jax
import jax.numpy as jnp
from jax import lax
from jax.experimental import pallas as pl
from jax.experimental.pallas import tpu as pltpu
from jax.sharding import PartitionSpec as P

MESH = pl.DeviceIdType.MESH
F32 = jnp.float32
BF16 = jnp.bfloat16
GROUP = 16
FIELDS = 5
HIDDEN = 64
PACK = 384
WIDE = 768
CHUNKS = 3
CHANNELS = 4 * FIELDS
EXTENDED = CHANNELS + 3


def pack(a, b):
    tail = jnp.concatenate([a[..., 128:192], b[..., 128:192]], axis=-1)
    return jnp.concatenate([a[..., 0:128], b[..., 0:128], tail], axis=-1)


def unpack(p):
    a = jnp.concatenate([p[..., 0:128], p[..., 256:320]], axis=-1)
    b = jnp.concatenate([p[..., 128:256], p[..., 320:384]], axis=-1)
    return a, b


def widen(v):
    return jnp.concatenate([v[:, 0:8], v[:, 8:16]], axis=-1)


def narrow(v):
    return jnp.concatenate([v[..., 0:PACK], v[..., PACK:WIDE]], axis=1)


def dot(a, b):
    return jnp.dot(a, b, preferred_element_type=F32)


def dot_t(a, b):
    return lax.dot_general(a, b, (((1,), (1,)), ((), ())), preferred_element_type=F32)


def iota(shape, axis):
    return lax.broadcasted_iota(jnp.int32, shape, axis)


def where_equal(shape, left, right):
    return jnp.where(left(iota(shape, 0)) == right(iota(shape, 1)), 1.0, 0.0)


def same(i):
    return i


def eighth(i):
    return i // 8


def step_kernel(
    scaling, s_hbm, c_hbm, x_ref, y_ref, z_ref, wit_ref, b_ref, wo_ref, bo_ref,
    ns_ref, sg_ref, total_ref,
    s_ref, c_ref, xt_ref, yt_ref, zt_ref, perm_ref, w1_ref, w1t_ref, w2_ref, w2t_ref,
    g1_ref, g2_ref, g3_ref, pay, slots, piece, ssem, rsem, lsem, msem, nsem, iosem,
    send, pen, recv, gx, gy, gz, cx, cy, cz, loc,
):
    me = lax.axis_index("space")
    team = lax.axis_index("dp")

    def shifted(s):
        return lax.rem(me // 4 + s % 4, 4) * 4 + lax.rem(me % 4 + s // 4, 4)

    def copy_of(phase, c, s, target):
        dst = shifted(s)
        return pltpu.make_async_remote_copy(
            src_ref=send.at[c, dst],
            dst_ref=target.at[c, me],
            send_sem=ssem.at[phase, c, s],
            recv_sem=rsem.at[phase, c, s],
            device_id={"space": dst},
            device_id_type=MESH,
        )

    def own_of(phase, c, target):
        return pltpu.make_async_copy(send.at[c, me], target.at[c, me], lsem.at[phase, c])

    def each(one):
        def run(s, carry):
            one(s)
            return carry

        lax.fori_loop(1, GROUP, run, 0)

    def start(phase, c, target):
        own_of(phase, c, target).start()
        each(lambda s: copy_of(phase, c, s, target).start())

    def finish(phase, c, target):
        own_of(phase, c, target).wait()
        each(lambda s: copy_of(phase, c, s, target).wait())

    def rows(c, half):
        return pl.ds(pl.multiple_of(c * 32 + 16 * half, 16), 16)

    def chunk(c):
        return pl.ds(pl.multiple_of(c * 32, 32), 32)

    def load_state(c):
        return pltpu.make_async_copy(
            s_hbm.at[:, :, chunk(c), :], s_ref.at[:, :, chunk(c), :], iosem.at[0, c]
        )

    def load_cotangent(c):
        return pltpu.make_async_copy(
            c_hbm.at[:, :, chunk(c), :], c_ref.at[:, :, chunk(c), :], iosem.at[1, c]
        )

    for c in range(CHUNKS):
        load_state(c).start()
    barrier = pltpu.get_barrier_semaphore()
    for axis, mine in (("space", me), ("dp", team)):

        def greet(s, axis=axis, mine=mine):
            pl.semaphore_signal(
                barrier, inc=1, device_id={axis: lax.rem(mine + s, GROUP)}, device_id_type=MESH
            )

        each(greet)
    perm_ref[...] = where_equal(
        (256, 256), lambda i: (i % 16) * 16 + i // 16, same
    ).astype(BF16)

    def pack_state(c):
        load_state(c).wait()
        for f in range(FIELDS):
            a = s_ref[f, :, rows(c, 0), :].reshape(256, 192)
            b = s_ref[f, :, rows(c, 1), :].reshape(256, 192)
            moved = dot(perm_ref[...], pack(a, b)).astype(BF16)
            send[c, :, :, f * PACK : (f + 1) * PACK] = moved.reshape(16, 16, PACK)

    def send_state(c, carry):
        pack_state(c)
        start(0, c, pen)
        return carry

    pack_state(0)
    pl.semaphore_wait(barrier, 2 * (GROUP - 1))
    start(0, 0, pen)
    lax.fori_loop(1, CHUNKS, send_state, 0)
    for c in range(CHUNKS):
        load_cotangent(c).start()

    for source, target in ((x_ref, xt_ref), (y_ref, yt_ref), (z_ref, zt_ref)):
        unit = where_equal(source.shape, same, same).astype(BF16)
        target[...] = dot_t(unit, source[...]).astype(BF16)

    def spread(w):
        n, m = w.shape
        left = where_equal((n * 8, n), eighth, same).astype(BF16)
        right = where_equal((m, m * 8), same, eighth).astype(BF16)
        return dot(left, dot(w, right).astype(BF16)) * diagonal((n * 8, m * 8))

    def diagonal(shape):
        return where_equal(shape, lambda i: i % 8, lambda i: i % 8)

    def turned(w):
        unit = where_equal((w.shape[1], w.shape[1]), same, same).astype(BF16)
        return dot_t(unit, w).astype(BF16)

    unit = where_equal((HIDDEN, HIDDEN), same, same)
    bias = jnp.sum(unit * b_ref[...], axis=1, keepdims=True)
    high = bias.astype(BF16).astype(F32)
    mid = (bias - high).astype(BF16).astype(F32)
    low = bias - high - mid
    places = iota((HIDDEN, EXTENDED * 8), 1) // 8
    right = where_equal((CHANNELS, EXTENDED * 8), same, eighth).astype(BF16)
    inner = dot(turned(wit_ref[...]), right)
    for place, column in enumerate((high, mid, low)):
        inner += jnp.where(places == CHANNELS + place, column, 0.0)
    left = where_equal((HIDDEN * 8, HIDDEN), eighth, same).astype(BF16)
    w1 = dot(left, inner.astype(BF16)) * diagonal((HIDDEN * 8, EXTENDED * 8))
    w1_ref[...] = w1.astype(BF16)
    w1t_ref[...] = spread(wit_ref[...]).astype(BF16)
    w2_ref[...] = spread(wo_ref[...]).astype(BF16)
    w2t_ref[...] = spread(turned(wo_ref[...])).astype(BF16)

    def lines(a, carry):
        for f in range(FIELDS):
            s = s_ref[f, a]
            dy = dot(y_ref[...], s).astype(BF16)
            dz = dot(s, zt_ref[...]).astype(BF16)
            for c in range(CHUNKS):
                lo, mid, hi = 32 * c, 32 * c + 16, 32 * c + 32
                gy[c, f, a] = pack(dy[lo:mid], dy[mid:hi])
                gz[c, f, a] = pack(dz[lo:mid], dz[mid:hi])
        return carry

    lax.fori_loop(0, GROUP, lines, 0)

    g1_ref[...] = jnp.zeros_like(g1_ref)
    g2_ref[...] = jnp.zeros_like(g2_ref)
    g3_ref[...] = jnp.zeros_like(g3_ref)

    def streamwise(c, operator):
        for f in range(FIELDS):
            lanes = slice(f * PACK, (f + 1) * PACK)
            done = dot(operator[...], pen[c, :, :, lanes].reshape(256, PACK)).astype(BF16)
            send[c, :, :, lanes] = done.reshape(16, 16, PACK)

    def forward_lines(c, carry):
        finish(0, c, pen)
        streamwise(c, x_ref)
        start(1, c, recv)
        return carry

    lax.fori_loop(0, CHUNKS, forward_lines, 0)

    def closure(c, a):
        state = pack(s_ref[:, a, rows(c, 0), :], s_ref[:, a, rows(c, 1), :])
        cot = pack(c_ref[:, a, rows(c, 0), :], c_ref[:, a, rows(c, 1), :])
        features = widen(
            jnp.concatenate([state, gx[:, a], gy[c, :, a], gz[c, :, a]], axis=0).astype(F32)
        )
        cw = widen(cot.astype(F32))
        ones = jnp.ones((3, 8, WIDE), F32)
        fb = jnp.concatenate([features, ones], axis=0).reshape(EXTENDED * 8, WIDE).astype(BF16)
        active = jnp.tanh(dot(w1_ref[...], fb))
        hidden = active.astype(BF16)
        closed = dot(w2_ref[...], hidden).reshape(FIELDS, 8, WIDE)
        half = 0.5 * cw
        d_closure = half.reshape(FIELDS * 8, WIDE).astype(BF16)
        d_hidden = dot(w2t_ref[...], d_closure)
        d_before = (d_hidden * (1.0 - active * active)).astype(BF16)
        d_features = dot(w1t_ref[...], d_before).reshape(CHANNELS, 8, WIDE)
        g1_ref[...] += dot_t(d_before, fb)
        g2_ref[...] += dot_t(hidden, d_closure)
        dc = d_closure.astype(F32)
        g3_ref[...] += sum(dc[:, 128 * t : 128 * (t + 1)] for t in range(WIDE // 128))
        u, v, w = features[0:1], features[1:2], features[2:3]
        fx, fy, fz = features[5:10], features[10:15], features[15:20]
        advect = u * fx + v * fy + w * fz
        bias = jnp.stack([jnp.full((8, WIDE), bo_ref[f], F32) for f in range(FIELDS)])
        updated = narrow(features[0:5] + 0.5 * (closed + bias - advect)).astype(BF16)
        first, second = unpack(updated)
        ns_ref[:, a, rows(c, 0), :] = first
        ns_ref[:, a, rows(c, 1), :] = second
        cx[:, a] = narrow(d_features[5:10] - half * u).astype(BF16)
        cy[c, :, a] = narrow(d_features[10:15] - half * v).astype(BF16)
        cz[c, :, a] = narrow(d_features[15:20] - half * w).astype(BF16)
        vel = [-jnp.sum(half * g, axis=0, keepdims=True) for g in (fx, fy, fz)]
        padded = jnp.concatenate(vel + [jnp.zeros((2, 8, WIDE), F32)], axis=0)
        loc[c, :, a] = narrow(cw + d_features[0:5] + padded)

    def backward_lines(c):
        finish(2, c, pen)
        streamwise(c, xt_ref)
        start(3, c, recv)

    def middle(c, carry):
        finish(1, c, recv)
        load_cotangent(c).wait()
        for f in range(FIELDS):
            lanes = slice(f * PACK, (f + 1) * PACK)
            back = dot(perm_ref[...], recv[c, :, :, lanes].reshape(256, PACK)).astype(BF16)
            gx[f] = back.reshape(16, 16, PACK)

        def plane(a, inner):
            closure(c, a)
            return inner

        lax.fori_loop(0, GROUP, plane, 0)
        for f in range(FIELDS):
            lanes = slice(f * PACK, (f + 1) * PACK)
            moved = dot(perm_ref[...], cx[f].reshape(256, PACK)).astype(BF16)
            send[c, :, :, lanes] = moved.reshape(16, 16, PACK)
        start(2, c, pen)

        @pl.when(c >= 1)
        def _():
            backward_lines(c - 1)

        return carry

    lax.fori_loop(0, CHUNKS, middle, 0)

    def folded(g):
        n, m = g.shape
        return jnp.sum((g[...] * diagonal((n, m))).reshape(n // 8, 8, m), axis=1)

    def summed(g, first):
        select = where_equal((40, g.shape[1]), same, lambda i: i // 8 + first)
        return lax.dot_general(
            select, folded(g), (((1,), (1,)), ((), ())),
            precision=lax.Precision.HIGHEST, preferred_element_type=F32,
        )

    pay[...] = jnp.zeros_like(pay)
    pay[0:40, 0:HIDDEN] = summed(g1_ref, 0) + summed(g2_ref, 32)
    out_bias = jnp.sum(g3_ref[...].reshape(FIELDS, 8, 128), axis=1)
    pay[40:48] = jnp.concatenate([out_bias, jnp.zeros((3, 128), F32)], axis=0)

    def eight(d):
        return pl.ds(pl.multiple_of(8 * d, 8), 8)

    def small(stage, s):
        axis, mine = (("space", me), ("dp", team), ("space", me))[stage]
        dst = lax.rem(mine + s, GROUP)
        source = pay.at[eight(dst)] if stage == 0 else piece.at[stage - 1]
        return pltpu.make_async_remote_copy(
            src_ref=source,
            dst_ref=slots.at[stage, mine],
            send_sem=msem.at[stage, s],
            recv_sem=nsem.at[stage, s],
            device_id={axis: dst},
            device_id_type=MESH,
        )

    def begin(stage):
        each(lambda s: small(stage, s).start())

    def collect(stage):
        each(lambda s: small(stage, s).wait())
        return sum(slots[stage, d] for d in range(1, GROUP)) + slots[stage, 0]

    slots[0, me] = pay[eight(me)]
    begin(0)

    def adjoint_lines(a, carry):
        for f in range(FIELDS):
            ys, zs = [], []
            for c in range(CHUNKS):
                ys += unpack(cy[c, f, a])
                zs += unpack(cz[c, f, a])
            total = dot(yt_ref[...], jnp.concatenate(ys, axis=0))
            total += dot(jnp.concatenate(zs, axis=0), z_ref[...])
            for c in range(CHUNKS):
                lo, mid, hi = 32 * c, 32 * c + 16, 32 * c + 32
                loc[c, f, a] += pack(total[lo:mid], total[mid:hi])
        return carry

    lax.fori_loop(0, GROUP, adjoint_lines, 0)
    over_space = collect(0)
    piece[0] = over_space
    slots[1, team] = over_space
    begin(1)
    backward_lines(CHUNKS - 1)
    over_all = collect(1) * scaling
    piece[1] = over_all
    slots[2, me] = over_all
    begin(2)

    def last(c, carry):
        finish(3, c, recv)
        for f in range(FIELDS):
            lanes = slice(f * PACK, (f + 1) * PACK)
            back = dot(perm_ref[...], recv[c, :, :, lanes].reshape(256, PACK))
            whole = (back.reshape(16, 16, PACK) + loc[c, f]).astype(BF16)
            first, second = unpack(whole)
            sg_ref[f, :, rows(c, 0), :] = first
            sg_ref[f, :, rows(c, 1), :] = second
        return carry

    lax.fori_loop(0, CHUNKS - 1, last, 0)
    each(lambda s: small(2, s).wait())
    for d in range(6):
        total_ref[8 * d : 8 * d + 8] = slots[2, d]
    last(CHUNKS - 1, 0)


def body(state, cotangent, x_operator, y_operator, z_operator, w_in, b_in, w_out, b_out):
    shape = state.shape[1:]
    vmem = pl.BlockSpec(memory_space=pltpu.VMEM)
    hbm = pl.BlockSpec(memory_space=pl.ANY)
    buffer = pltpu.VMEM((CHUNKS, GROUP, GROUP, FIELDS * PACK), BF16)
    packed = pltpu.VMEM((CHUNKS, FIELDS, GROUP, GROUP, PACK), BF16)
    part = pltpu.VMEM((FIELDS, GROUP, GROUP, PACK), BF16)
    whole = pltpu.VMEM(shape, BF16)
    dma = pltpu.SemaphoreType.DMA
    cells = (
        lax.axis_size("dp") * lax.axis_size("space") * shape[1] * shape[2] * shape[3]
    )
    ns, sg, total = pl.pallas_call(
        functools.partial(step_kernel, 1.0 / math.sqrt(cells)),
        out_shape=(
            pltpu.VMEM(shape, BF16),
            pltpu.VMEM(shape, BF16),
            pltpu.VMEM((48, 128), F32),
        ),
        in_specs=[hbm] * 2 + [vmem] * 6 + [pl.BlockSpec(memory_space=pltpu.SMEM)],
        out_specs=[vmem] * 3,
        scratch_shapes=[
            whole, whole,
            pltpu.VMEM(x_operator.shape, BF16),
            pltpu.VMEM(y_operator.shape, BF16),
            pltpu.VMEM(z_operator.shape, BF16),
            pltpu.VMEM((256, 256), BF16),
            pltpu.VMEM((HIDDEN * 8, EXTENDED * 8), BF16),
            pltpu.VMEM((CHANNELS * 8, HIDDEN * 8), BF16),
            pltpu.VMEM((FIELDS * 8, HIDDEN * 8), BF16),
            pltpu.VMEM((HIDDEN * 8, FIELDS * 8), BF16),
            pltpu.VMEM((HIDDEN * 8, EXTENDED * 8), F32),
            pltpu.VMEM((HIDDEN * 8, FIELDS * 8), F32),
            pltpu.VMEM((FIELDS * 8, 128), F32),
            pltpu.VMEM((128, 128), F32),
            pltpu.VMEM((3, GROUP, 8, 128), F32),
            pltpu.VMEM((2, 8, 128), F32),
            dma((4, CHUNKS, GROUP)),
            dma((4, CHUNKS, GROUP)),
            dma((4, CHUNKS)),
            dma((3, GROUP)),
            dma((3, GROUP)),
            dma((2, CHUNKS)),
            buffer, buffer, buffer, part, packed, packed, part, packed, packed,
            pltpu.VMEM((CHUNKS, FIELDS, GROUP, GROUP, PACK), F32),
        ],
        compiler_params=pltpu.CompilerParams(
            collective_id=0, has_side_effects=True, vmem_limit_bytes=52 * 1024 * 1024
        ),
        cost_estimate=pl.CostEstimate(
            flops=10**11, bytes_accessed=2 * 10**7, transcendentals=2 * 10**7
        ),
        name="evolution",
    )(
        state[0], cotangent[0], x_operator, y_operator, z_operator,
        w_in.T, b_in[None, :], w_out, b_out,
    )
    return (
        ns[None],
        sg[None],
        total[0:CHANNELS, 0:HIDDEN].T,
        total[CHANNELS, 0:HIDDEN],
        total[32 : 32 + FIELDS, 0:HIDDEN],
        jnp.sum(total[40 : 40 + FIELDS], axis=1),
    )


def solution(mesh):
    wide = P("dp", None, "space", None, None)
    return jax.shard_map(
        body,
        mesh=mesh,
        in_specs=(wide, wide) + (P(),) * 7,
        out_specs=(wide, wide) + (P(),) * 4,
        check_vma=False,
    )
```
